32 devices in a mesh: groups: 2 (over y), ops: 16 (over z, x, core).
Axes of the slice: x: 2, y: 2, z: 4, core: 2. Of those that a mesh axis runs over, the one named last changes fastest.
Arguments:
- psi_start: float32 [1024, 128], P(('groups', 'ops')), parts along dimension 0, may hold values from -6 to 6
- precond: float32 [1024, 128], P(('groups', 'ops')), parts along dimension 0, may hold values from 0.02 to 0.2
- left_ops: bfloat16 [512, 64, 64], P(('groups', 'ops')), parts along dimension 0, may hold values from -0.1875 to 0.1875
- right_ops: bfloat16 [512, 128, 128], P(('groups', 'ops')), parts along dimension 0, may hold values from -0.5 to 0.5
- term_in: int32 [512, 16], P(('groups', 'ops')), parts along dimension 0, may hold values from 0 to 7
- term_out: int32 [512, 16], P(('groups', 'ops')), parts along dimension 0, may hold values from 0 to 7
- term_live: int32 [32], P(('groups', 'ops')), parts along dimension 0, may hold values from 1 to 16, as said below
- left_rot: float32 [1024, 64], P(('groups', 'ops')), parts along dimension 0, may hold values from -0.75 to 0.75
Outputs:
- start_energy: float32 [2], P('groups'), parts along dimension 0
- energies: float32 [6], P('groups'), parts along dimension 0
- shifted: float32 [1024, 128], P(('groups', 'ops')), parts along dimension 0
The draws below stay inside these ranges and needn't reach their ends.
There are 2 independent parts, one for each index of `groups`. The reference program is written for one: setup_inputs(seed, part) draws one part's arguments, and reference() takes and returns one part's arrays. A program takes and returns all parts, laid end to end along the dimension named above; each array names one. Nothing has to cross between parts.
Inputs may be any that keep to these rules, and one draw needn't show every extreme that they name: `term_live`: some index of ops has all 16 slots live in every draw.
All inputs are finite; a program needn't handle non-finite values.
Results may differ from the reference program's by a relative error of at most 0.011.
Values may be sent and summed in bfloat16 or wider, within the bound.
A program may use at most 64 MiB of HBM per device.

```python
import math
import jax
import jax.numpy as jnp
from jax import lax

BL = 64
BR = 128
KEPT = 64
TERM_DEV = 16
PAIRS = 16
ITERS = 4
SECTORS = 8
ROWS = 512
TERMS = 256
N_OPS = 16


def draw_term_live(key, part):
    key = jax.random.fold_in(key, 7)
    first, second = jax.random.split(key)
    counts = jax.random.randint(first, (N_OPS,), 1, TERM_DEV + 1)
    where = jax.random.randint(second, (), 0, N_OPS)
    return counts.at[where].set(TERM_DEV).astype(jnp.int32)


def plant(entries, stream_key, low, largest):
    extent = entries.shape
    spot = [jax.random.randint(jax.random.fold_in(stream_key, axis), (), 0, extent[axis]) for axis in range(len(extent))]
    entries = entries.at[tuple(spot)].set(low)
    longest = extent.index(max(extent))
    spot[longest] = (spot[longest] + 1) % extent[longest]
    return entries.at[tuple(spot)].set(largest)


def levels(stream_key, dims, shards, least, high):
    factor_of, own = 1.0, jax.random.fold_in(stream_key, 6)
    for axis_at, blocks in shards:
        draws = jnp.exp(jax.random.uniform(jax.random.fold_in(own, axis_at), (blocks,), jnp.float32, least / len(shards), high / len(shards)))
        factor_of = factor_of * jnp.repeat(draws, dims[axis_at] // blocks).reshape([-1 if axis == axis_at else 1 for axis in range(len(dims))])
    return factor_of


def noise(rng, dims, scale, limit, cuts=(), kind=jnp.bfloat16):
    entries = jax.random.normal(rng, dims, jnp.float32) * scale
    if len(cuts) > 0:
        entries = levels(rng, dims, cuts, -0.22, 0.18) * entries
    return jnp.clip(entries, min=-limit, max=limit).astype(kind)


def setup_inputs(seed: int = 0, part: int = 0) -> dict:
    seeds = jax.random.split(jax.random.key(seed), 9)
    part_keys = jax.random.split(jax.random.fold_in(seeds[8], part), 9)
    psi_start = noise(part_keys[0], (ROWS, BR), 1.0, 6.0, ((0, 16),), jnp.float32)
    precond = jnp.clip(jnp.exp(math.log(0.2) - 2.3025851 * jax.random.uniform(part_keys[1], (ROWS, BR), jnp.float32) ** levels(part_keys[1], (ROWS, BR), ((0, 16),), -0.2, 0.2)), 0.02, 0.2)
    left_ops = noise(part_keys[2], (TERMS, BL, BL), (BL * 16) ** -0.5, 0.1875, ((0, 16),))
    right_ops = noise(part_keys[3], (TERMS, BR, BR), BR ** -0.5, 0.5, ((0, 16),))
    term_in = plant(jax.random.randint(part_keys[4], (TERMS, PAIRS), 0, SECTORS), jax.random.fold_in(part_keys[4], 1), 0, SECTORS - 1).astype(jnp.int32)
    term_out = plant(jax.random.randint(part_keys[5], (TERMS, PAIRS), 0, SECTORS), jax.random.fold_in(part_keys[5], 1), 0, SECTORS - 1).astype(jnp.int32)
    term_live = draw_term_live(jax.random.fold_in(jax.random.fold_in(seeds[8], part), 71), part)
    left_rot = noise(part_keys[7], (ROWS, KEPT), BL ** -0.5, 0.75, ((0, 16),), jnp.float32)
    return dict(psi_start=psi_start, precond=precond, left_ops=left_ops, right_ops=right_ops, term_in=term_in, term_out=term_out, term_live=term_live, left_rot=left_rot)


def apply_terms(xb, left_ops, right_ops, term_in, term_out, live_slot):
    blocks = xb.reshape(SECTORS, BL, BR)
    start = jnp.zeros((SECTORS, BL, BR), jnp.float32)

    def step(total, item):
        left, right, ins, outs, alive = item

        def add(acc):
            chosen = blocks[ins].astype(jnp.float32)
            inner = jnp.einsum('ab,pbc->pac', left.astype(jnp.float32), chosen).astype(jnp.bfloat16)
            image = jnp.einsum('pac,dc->pad', inner.astype(jnp.float32), right.astype(jnp.float32))
            return acc.at[outs].add(image)
        return (lax.cond(alive, add, lambda acc: acc, total), None)
    total, unused = lax.scan(step, start, (left_ops, right_ops, term_in, term_out, live_slot))
    return total.reshape(ROWS, BR)

def reference(psi_start, precond, left_ops, right_ops, term_in, term_out, term_live, left_rot):
    live_slot = (jnp.arange(TERM_DEV, dtype=jnp.int32)[None, :] < term_live[:, None]).reshape(-1)
    vector = psi_start
    found = []
    for step_index in range(ITERS):
        image = apply_terms(vector.astype(jnp.bfloat16), left_ops, right_ops, term_in, term_out, live_slot)
        quotient = jnp.sum(vector * image) / jnp.sum(vector * vector)
        found.append(quotient)
        update = vector - precond * (image - quotient * vector)
        vector = update / jnp.sqrt(jnp.mean(update * update) + 1e-06)
    rot_blocks = left_rot.reshape(SECTORS, BL, KEPT)
    shifted = jnp.einsum('sbk,sbc->skc', rot_blocks, vector.reshape(SECTORS, BL, BR), precision=lax.Precision.HIGHEST)
    first = jnp.stack(found[:1]).astype(jnp.float32)
    later = jnp.stack(found[1:]).astype(jnp.float32)
    return (first, later, shifted.reshape(SECTORS * KEPT, BR))
```

```python
import functools
import jax
import jax.numpy as jnp
from jax import lax
from jax.experimental import pallas as pl
from jax.experimental.pallas import tpu as pltpu
from jax.sharding import PartitionSpec as P

ITERS = 4
SUB = 16
F32 = jnp.float32
BF16 = jnp.bfloat16


def from_partner(block, axis, stride):
    count = lax.axis_size(axis)
    route = []
    for low in range(count):
        high = low | 1 << stride
        if high != low and high < count:
            route += [(low, high), (high, low)]
    return lax.ppermute(block, axis, route)


def local_terms(whole_b, left_ops, right_ops, term_in, term_out, live_count):
    block_rows = left_ops.shape[1]
    width = whole_b.shape[1]
    sector_count = whole_b.shape[0] // block_rows
    slot_count = left_ops.shape[0]
    pair_count = term_in.shape[1]
    blocks = whole_b.reshape(sector_count, block_rows, width)
    chosen = blocks[term_in]
    inner = jnp.einsum(
        "tab,tpbc->tpac", left_ops, chosen, preferred_element_type=F32
    ).astype(BF16)
    image = jnp.einsum("tpac,tdc->tpad", inner, right_ops, preferred_element_type=F32)
    alive = jnp.arange(slot_count, dtype=jnp.int32) < live_count
    onehot = (
        term_out[:, :, None] == jnp.arange(sector_count, dtype=jnp.int32)[None, None, :]
    ) & alive[:, None, None]
    onehot = onehot.astype(F32).reshape(slot_count * pair_count, sector_count)
    flat = image.reshape(slot_count * pair_count, block_rows * width)
    total = jnp.dot(
        onehot.T, flat, precision=lax.Precision.HIGHEST, preferred_element_type=F32
    )
    return total.reshape(whole_b.shape[0], width)


def pair_body(psi_start, precond, left_ops, right_ops, term_in, term_out, term_live, left_rot):
    live_count = term_live[0]
    own_rows = psi_start.shape[0]
    offset = lax.axis_index("ops") * own_rows
    found = []
    vector, scaling = (
        lax.all_gather(psi_start, "ops", axis=0, tiled=True),
        lax.all_gather(precond, "ops", axis=0, tiled=True),
    )
    for step_index in range(ITERS):
        terms = local_terms(
            vector.astype(BF16), left_ops, right_ops, term_in, term_out, live_count
        )
        image = lax.psum(terms, "ops")
        quotient = jnp.sum(vector * image) / jnp.sum(vector * vector)
        found.append(quotient)
        update = vector - scaling * (image - quotient * vector)
        vector = update / jnp.sqrt(jnp.mean(update * update) + 1e-06)
    mine = lax.dynamic_slice_in_dim(vector, offset, own_rows, 0)
    partial_value = jnp.dot(
        left_rot.T, mine, precision=lax.Precision.HIGHEST, preferred_element_type=F32
    )
    half = partial_value.shape[0] // 2
    parity = lax.axis_index("ops") % 2
    keep_part = lax.dynamic_slice_in_dim(partial_value, parity * half, half, 0)
    give_part = lax.dynamic_slice_in_dim(partial_value, (1 - parity) * half, half, 0)
    received = from_partner(give_part, "ops", 0)
    return (jnp.stack(found[:1]), jnp.stack(found[1:]), keep_part + received)


def iota(shape, dim):
    return lax.broadcasted_iota(jnp.int32, shape, dim)


def kernel(
    n,
    live_ref, psi_ref, pre_ref, left_ref, right_ref, tin_ref, tout_ref, rot_ref,
    first_ref, later_ref, out_ref,
    counts, inner, image, xsend, xbuf, rsend, rbuf, qsend, qbuf, usend, ubuf, part, got,
    x_out, x_in, r_out, r_in, q_out, q_in, u_out, u_in, p_out, p_in,
):
    me = lax.axis_index("ops")
    slots, bl = left_ref.shape[0], left_ref.shape[1]
    br = right_ref.shape[1]
    pairs = tin_ref.shape[1]
    own = psi_ref.shape[0]
    per = bl // own
    sectors = n // per
    deep = bl // SUB
    st = sectors * SUB
    entries = n * own * br

    barrier = pltpu.get_barrier_semaphore()

    def greet(k, carry):
        pl.semaphore_signal(barrier, inc=1, device_id={"ops": lax.rem(me + k, n)},
                            device_id_type=pl.DeviceIdType.MESH)
        return carry

    lax.fori_loop(1, n, greet, 0)

    def copy(src, dst, out_sem, in_sem, to):
        return pltpu.make_async_remote_copy(
            src_ref=src, dst_ref=dst, send_sem=out_sem, recv_sem=in_sem,
            device_id={"ops": to}, device_id_type=pl.DeviceIdType.MESH)

    def x_copy(i, to, slot):
        return copy(xsend.at[i], xbuf.at[i, slot], x_out.at[i, to], x_in.at[i, slot], to)

    def u_copy(i, to, slot):
        return copy(usend.at[i], ubuf.at[i, slot], u_out.at[i, to], u_in.at[i, slot], to)

    def r_copy(i, to, slot):
        return copy(rsend.at[i, to], rbuf.at[i, slot], r_out.at[i, to], r_in.at[i, slot], to)

    def q_copy(i, to, slot):
        return copy(qsend.at[i], qbuf.at[i, slot], q_out.at[i, to], q_in.at[i, slot], to)

    def each(act):
        def one(k, carry):
            act(lax.rem(me + k, n))
            return carry
        lax.fori_loop(1, n, one, 0)

    def start(makers, i):
        def act(to):
            for make in makers:
                make(i, to, me).start()
        each(act)

    def arrive(makers, i):
        def act(frm):
            for make in makers:
                make(i, frm, frm).wait_recv()
        each(act)

    def sent(makers, i):
        def act(to):
            for make in makers:
                make(i, to, me).wait_send()
        each(act)

    def offer(i, u, extra):
        rows = jnp.concatenate([jnp.sum(u * u, axis=0, keepdims=True), extra], axis=0)
        usend[i] = rows
        ubuf[i, me] = rows

    def offer_x(i, ub):
        xsend[i] = ub
        xbuf[i, me] = ub

    def build_counts():
        live = live_ref[0]
        flat = slots * pairs
        row, col = iota((flat, slots), 0), iota((flat, slots), 1)
        spread = (row // pairs == col).astype(BF16)
        prow, pcol = iota((flat, pairs), 0), iota((flat, pairs), 1)
        ins = jnp.dot(spread, tin_ref[...].astype(F32).astype(BF16), preferred_element_type=F32)
        ins = jnp.sum(jnp.where(prow % pairs == pcol, ins, 0.0), axis=1, keepdims=True)
        outs = lax.dot_general(tout_ref[...].astype(F32).astype(BF16), spread,
                               (((0,), (1,)), ((), ())), preferred_element_type=F32)
        orow, ocol = iota((pairs, flat), 0), iota((pairs, flat), 1)
        outs = jnp.sum(jnp.where(ocol % pairs == orow, outs, 0.0), axis=0, keepdims=True)
        target = (iota((st, flat), 0) // SUB).astype(F32)
        goes = (outs == target).astype(F32).astype(BF16)
        slot = iota((flat, st), 0) // pairs
        sector = (iota((flat, st), 1) // SUB).astype(F32)
        comes = jnp.where(ins == sector, 1.0, 0.0)
        comes = jnp.where(slot < live, comes, 0.0)
        same = (iota((st, st), 0) % SUB == iota((st, st), 1) % SUB).astype(F32)
        for j in range(slots):
            these = jnp.where(slot == j, comes, 0.0).astype(BF16)
            c = jnp.dot(goes, these, preferred_element_type=F32) * same
            c = c.astype(BF16)
            counts[:, 2 * j * st:(2 * j + 1) * st] = c
            counts[:, (2 * j + 1) * st:(2 * j + 2) * st] = c

    def apply(i):
        blocks = [xbuf[i, t * per:(t + 1) * per].reshape(bl, br) for t in range(sectors)]
        x = jnp.concatenate(blocks, axis=1)
        inner[...] = jnp.dot(left_ref[...].reshape(slots * bl, bl), x,
                             preferred_element_type=F32).astype(BF16)
        for j in range(slots):
            y = jnp.concatenate(
                [inner[j * bl:(j + 1) * bl, s * br:(s + 1) * br] for s in range(sectors)], axis=0)
            z = lax.dot_general(y, right_ref[j], (((1,), (1,)), ((), ())),
                                preferred_element_type=F32)
            hi = z.astype(BF16)
            lo = (z - hi.astype(F32)).astype(BF16)
            for which, value in enumerate((hi, lo)):
                top = (2 * j + which) * st
                for a in range(deep):
                    image[top:top + st, a * br:(a + 1) * br] = jnp.concatenate(
                        [value[s * bl + a * SUB:s * bl + (a + 1) * SUB] for s in range(sectors)],
                        axis=0)
        return jnp.dot(counts[...], image[...], preferred_element_type=F32)

    v = psi_ref[...]
    ub = v.astype(BF16)
    offer_x(0, ub)
    offer(0, v, jnp.zeros((1, br), F32))
    pl.semaphore_wait(barrier, n - 1)
    start((x_copy, u_copy), 0)
    build_counts()
    pre = pre_ref[...]
    scale = jnp.ones((1, 1), F32)
    u = v
    overlap = jnp.zeros((1, 1), F32)
    square = overlap

    def total(rows):
        return jnp.sum(rows, axis=1, keepdims=True)

    for i in range(ITERS + 1):
        if i < ITERS:
            arrive((x_copy, u_copy), i)
        else:
            arrive((u_copy,), i)
        rows = jnp.sum(ubuf[i], axis=0)
        usq = total(rows[0:1])
        if i > 0:
            quotient = (overlap + total(rows[1:2])) / square
            if i == 1:
                first_ref[0] = jnp.sum(quotient)
            else:
                later_ref[i - 2] = jnp.sum(quotient)
            scale = lax.rsqrt(usq * (1.0 / entries) + 1e-06)
        if i == ITERS:
            break
        v = u * scale
        square = usq * scale * scale
        acc = apply(i)
        dots = jnp.zeros((own, br), F32)
        for o in range(n):
            t, h = o // per, o % per
            steps = own // SUB
            piece = jnp.concatenate(
                [acc[t * SUB:(t + 1) * SUB, (h * steps + a) * br:(h * steps + a + 1) * br]
                 for a in range(steps)], axis=0)
            rsend[i, o] = piece.astype(BF16)
            dots = dots + piece * xbuf[i, o].astype(F32)
        row = jnp.sum(dots, axis=0, keepdims=True)
        qsend[i] = row
        qbuf[i, me] = row
        rbuf[i, me] = rsend[i, me]
        start((r_copy, q_copy), i)
        arrive((r_copy, q_copy), i)
        w = jnp.zeros((own, br), F32)
        for o in range(n):
            w = w + rbuf[i, o].astype(F32)
        w = w * scale
        overlap = total(jnp.sum(qbuf[i], axis=0)) * scale * scale
        q = overlap / square
        missing = jnp.sum((v - scale * ub.astype(F32)) * w, axis=0, keepdims=True)
        u = v - pre * (w - q * v)
        ub = u.astype(BF16)
        offer(i + 1, u, missing)
        if i + 1 < ITERS:
            offer_x(i + 1, ub)
            start((x_copy, u_copy), i + 1)
        else:
            start((u_copy,), i + 1)
            part[...] = lax.dot_general(
                rot_ref[...], u, (((0,), (0,)), ((), ())),
                precision=lax.Precision.HIGHEST, preferred_element_type=F32)
            parity = lax.rem(me, 2)
            half = part.shape[0] // 2
            give = copy(part.at[pl.ds(pl.multiple_of((1 - parity) * half, half), half)],
                        got, p_out, p_in, me + 1 - 2 * parity)
            give.start()

    give.wait_recv()
    keep = part[pl.ds(pl.multiple_of(parity * half, half), half)]
    out_ref[...] = (keep + got[...]) * scale
    give.wait_send()
    for i in range(ITERS):
        sent((x_copy, u_copy, r_copy, q_copy), i)
    sent((u_copy,), ITERS)


def dense_body(psi_start, precond, left_ops, right_ops, term_in, term_out, term_live, left_rot):
    n = lax.axis_size("ops")
    slots, bl = left_ops.shape[0], left_ops.shape[1]
    own, br = psi_start.shape
    kept = left_rot.shape[1]
    sectors = n * own // bl
    st = sectors * SUB
    vmem = pl.BlockSpec(memory_space=pltpu.VMEM)
    smem = pl.BlockSpec(memory_space=pltpu.SMEM)
    dma = pltpu.SemaphoreType.DMA
    return pl.pallas_call(
        functools.partial(kernel, n),
        out_shape=(
            jax.ShapeDtypeStruct((1,), F32),
            jax.ShapeDtypeStruct((ITERS - 1,), F32),
            jax.ShapeDtypeStruct((kept // 2, br), F32),
        ),
        in_specs=[smem] + [vmem] * 7,
        out_specs=(smem, smem, vmem),
        scratch_shapes=[
            pltpu.VMEM((st, slots * 2 * st), BF16),
            pltpu.VMEM((slots * bl, sectors * br), BF16),
            pltpu.VMEM((slots * 2 * st, bl // SUB * br), BF16),
            pltpu.VMEM((ITERS, own, br), BF16),
            pltpu.VMEM((ITERS, n, own, br), BF16),
            pltpu.VMEM((ITERS, n, own, br), BF16),
            pltpu.VMEM((ITERS, n, own, br), BF16),
            pltpu.VMEM((ITERS, 1, br), F32),
            pltpu.VMEM((ITERS, n, 1, br), F32),
            pltpu.VMEM((ITERS + 1, 2, br), F32),
            pltpu.VMEM((ITERS + 1, n, 2, br), F32),
            pltpu.VMEM((kept, br), F32),
            pltpu.VMEM((kept // 2, br), F32),
            dma((ITERS, n)), dma((ITERS, n)), dma((ITERS, n)), dma((ITERS, n)),
            dma((ITERS, n)), dma((ITERS, n)), dma((ITERS + 1, n)), dma((ITERS + 1, n)),
            dma, dma,
        ],
        compiler_params=pltpu.CompilerParams(
            collective_id=0, has_side_effects=True, vmem_limit_bytes=40 * 2**20),
    )(term_live, psi_start, precond, left_ops, right_ops, term_in, term_out, left_rot)


def body(psi_start, precond, left_ops, right_ops, term_in, term_out, term_live, left_rot):
    n = lax.axis_size("ops")
    own = psi_start.shape[0]
    bl = left_ops.shape[1]
    sectors = n * own // bl
    dense = sectors <= term_in.shape[1] and own % SUB == 0 and bl == 2 * own
    run = dense_body if dense else pair_body
    return run(psi_start, precond, left_ops, right_ops, term_in, term_out, term_live, left_rot)


def solution(mesh):
    rows = P(("groups", "ops"), None)
    blocks = P(("groups", "ops"), None, None)
    return jax.shard_map(
        body,
        mesh=mesh,
        in_specs=(rows, rows, blocks, blocks, rows, rows, P(("groups", "ops")), rows),
        out_specs=(P("groups"), P("groups"), rows),
        check_vma=False,
    )
```

```python
import functools
import jax
import jax.numpy as jnp
from jax import lax
from jax.experimental import pallas as pl
from jax.experimental.pallas import tpu as pltpu
from jax.sharding import PartitionSpec as P

ITERS = 4
SUB = 16
F32 = jnp.float32
BF16 = jnp.bfloat16


def from_partner(block, axis, stride):
    count = lax.axis_size(axis)
    route = []
    for low in range(count):
        high = low | 1 << stride
        if high != low and high < count:
            route += [(low, high), (high, low)]
    return lax.ppermute(block, axis, route)


def local_terms(whole_b, left_ops, right_ops, term_in, term_out, live_count):
    block_rows = left_ops.shape[1]
    width = whole_b.shape[1]
    sector_count = whole_b.shape[0] // block_rows
    slot_count = left_ops.shape[0]
    pair_count = term_in.shape[1]
    blocks = whole_b.reshape(sector_count, block_rows, width)
    chosen = blocks[term_in]
    inner = jnp.einsum(
        "tab,tpbc->tpac", left_ops, chosen, preferred_element_type=F32
    ).astype(BF16)
    image = jnp.einsum("tpac,tdc->tpad", inner, right_ops, preferred_element_type=F32)
    alive = jnp.arange(slot_count, dtype=jnp.int32) < live_count
    onehot = (
        term_out[:, :, None] == jnp.arange(sector_count, dtype=jnp.int32)[None, None, :]
    ) & alive[:, None, None]
    onehot = onehot.astype(F32).reshape(slot_count * pair_count, sector_count)
    flat = image.reshape(slot_count * pair_count, block_rows * width)
    total = jnp.dot(
        onehot.T, flat, precision=lax.Precision.HIGHEST, preferred_element_type=F32
    )
    return total.reshape(whole_b.shape[0], width)


def pair_body(psi_start, precond, left_ops, right_ops, term_in, term_out, term_live, left_rot):
    live_count = term_live[0]
    own_rows = psi_start.shape[0]
    offset = lax.axis_index("ops") * own_rows
    found = []
    vector, scaling = (
        lax.all_gather(psi_start, "ops", axis=0, tiled=True),
        lax.all_gather(precond, "ops", axis=0, tiled=True),
    )
    for step_index in range(ITERS):
        terms = local_terms(
            vector.astype(BF16), left_ops, right_ops, term_in, term_out, live_count
        )
        image = lax.psum(terms, "ops")
        quotient = jnp.sum(vector * image) / jnp.sum(vector * vector)
        found.append(quotient)
        update = vector - scaling * (image - quotient * vector)
        vector = update / jnp.sqrt(jnp.mean(update * update) + 1e-06)
    mine = lax.dynamic_slice_in_dim(vector, offset, own_rows, 0)
    partial_value = jnp.dot(
        left_rot.T, mine, precision=lax.Precision.HIGHEST, preferred_element_type=F32
    )
    half = partial_value.shape[0] // 2
    parity = lax.axis_index("ops") % 2
    keep_part = lax.dynamic_slice_in_dim(partial_value, parity * half, half, 0)
    give_part = lax.dynamic_slice_in_dim(partial_value, (1 - parity) * half, half, 0)
    received = from_partner(give_part, "ops", 0)
    return (jnp.stack(found[:1]), jnp.stack(found[1:]), keep_part + received)


def iota(shape, dim):
    return lax.broadcasted_iota(jnp.int32, shape, dim)


def kernel(
    n,
    live_ref, psi_hbm, tin_hbm, tout_hbm, left_hbm, right_hbm, pre_hbm, rot_hbm,
    first_ref, later_ref, out_ref,
    psi_ref, tin_ref, tout_ref, left_ref, right_ref, pre_ref, rot_ref, load,
    counts, inner, image, xsend, xbuf, rsend, rbuf, qsend, qbuf, usend, ubuf, part, got,
    x_out, x_in, r_out, r_in, q_out, q_in, u_out, u_in, p_out, p_in,
):
    me = lax.axis_index("ops")
    slots, bl = left_ref.shape[0], left_ref.shape[1]
    br = right_ref.shape[1]
    pairs = tin_ref.shape[1]
    own = psi_ref.shape[0]
    per = bl // own
    sectors = n // per
    deep = bl // SUB
    st = sectors * SUB
    entries = n * own * br

    barrier = pltpu.get_barrier_semaphore()

    def greet(k, carry):
        pl.semaphore_signal(barrier, inc=1, device_id={"ops": lax.rem(me + k, n)},
                            device_id_type=pl.DeviceIdType.MESH)
        return carry

    loads = [
        pltpu.make_async_copy(src, dst, load.at[k])
        for k, (src, dst) in enumerate((
            (psi_hbm, psi_ref), (tin_hbm, tin_ref), (tout_hbm, tout_ref), (left_hbm, left_ref),
            (right_hbm, right_ref), (pre_hbm, pre_ref), (rot_hbm, rot_ref)))
    ]
    for one_load in loads:
        one_load.start()
    lax.fori_loop(1, n, greet, 0)

    def copy(src, dst, out_sem, in_sem, to):
        return pltpu.make_async_remote_copy(
            src_ref=src, dst_ref=dst, send_sem=out_sem, recv_sem=in_sem,
            device_id={"ops": to}, device_id_type=pl.DeviceIdType.MESH)

    def x_copy(i, to, slot):
        return copy(xsend.at[i], xbuf.at[i, slot], x_out.at[i, to], x_in.at[i, slot], to)

    def u_copy(i, to, slot):
        return copy(usend.at[i], ubuf.at[i, slot], u_out.at[i, to], u_in.at[i, slot], to)

    def r_copy(i, to, slot):
        return copy(rsend.at[i, to], rbuf.at[i, slot], r_out.at[i, to], r_in.at[i, slot], to)

    def q_copy(i, to, slot):
        return copy(qsend.at[i], qbuf.at[i, slot], q_out.at[i, to], q_in.at[i, slot], to)

    def each(act):
        def one(k, carry):
            act(lax.rem(me + k, n))
            return carry
        lax.fori_loop(1, n, one, 0)

    def start(makers, i):
        def act(to):
            for make in makers:
                make(i, to, me).start()
        each(act)

    def arrive(makers, i):
        def act(frm):
            for make in makers:
                make(i, frm, frm).wait_recv()
        each(act)

    def sent(makers, i):
        def act(to):
            for make in makers:
                make(i, to, me).wait_send()
        each(act)

    def offer(i, u, extra):
        rows = jnp.concatenate([jnp.sum(u * u, axis=0, keepdims=True), extra], axis=0)
        usend[i] = rows
        ubuf[i, me] = rows

    def offer_x(i, ub):
        xsend[i] = ub
        xbuf[i, me] = ub

    def build_counts():
        live = live_ref[0]
        flat = slots * pairs
        row, col = iota((flat, slots), 0), iota((flat, slots), 1)
        spread = (row // pairs == col).astype(BF16)
        prow, pcol = iota((flat, pairs), 0), iota((flat, pairs), 1)
        ins = jnp.dot(spread, tin_ref[...].astype(F32).astype(BF16), preferred_element_type=F32)
        ins = jnp.sum(jnp.where(prow % pairs == pcol, ins, 0.0), axis=1, keepdims=True)
        outs = lax.dot_general(tout_ref[...].astype(F32).astype(BF16), spread,
                               (((0,), (1,)), ((), ())), preferred_element_type=F32)
        orow, ocol = iota((pairs, flat), 0), iota((pairs, flat), 1)
        outs = jnp.sum(jnp.where(ocol % pairs == orow, outs, 0.0), axis=0, keepdims=True)
        target = (iota((st, flat), 0) // SUB).astype(F32)
        goes = (outs == target).astype(F32).astype(BF16)
        slot = iota((flat, st), 0) // pairs
        sector = (iota((flat, st), 1) // SUB).astype(F32)
        comes = jnp.where(ins == sector, 1.0, 0.0)
        comes = jnp.where(slot < live, comes, 0.0)
        same = (iota((st, st), 0) % SUB == iota((st, st), 1) % SUB).astype(F32)
        for j in range(slots):
            these = jnp.where(slot == j, comes, 0.0).astype(BF16)
            c = jnp.dot(goes, these, preferred_element_type=F32) * same
            c = c.astype(BF16)
            counts[:, 2 * j * st:(2 * j + 1) * st] = c
            counts[:, (2 * j + 1) * st:(2 * j + 2) * st] = c

    def apply(i):
        blocks = [xbuf[i, t * per:(t + 1) * per].reshape(bl, br) for t in range(sectors)]
        x = jnp.concatenate(blocks, axis=1)
        inner[...] = jnp.dot(left_ref[...].reshape(slots * bl, bl), x,
                             preferred_element_type=F32).astype(BF16)
        for j in range(slots):
            y = jnp.concatenate(
                [inner[j * bl:(j + 1) * bl, s * br:(s + 1) * br] for s in range(sectors)], axis=0)
            z = lax.dot_general(y, right_ref[j], (((1,), (1,)), ((), ())),
                                preferred_element_type=F32)
            hi = z.astype(BF16)
            lo = (z - hi.astype(F32)).astype(BF16)
            for which, value in enumerate((hi, lo)):
                top = (2 * j + which) * st
                for a in range(deep):
                    image[top:top + st, a * br:(a + 1) * br] = jnp.concatenate(
                        [value[s * bl + a * SUB:s * bl + (a + 1) * SUB] for s in range(sectors)],
                        axis=0)
        return jnp.dot(counts[...], image[...], preferred_element_type=F32)

    loads[0].wait()
    v = psi_ref[...]
    ub = v.astype(BF16)
    offer_x(0, ub)
    offer(0, v, jnp.zeros((1, br), F32))
    pl.semaphore_wait(barrier, n - 1)
    start((x_copy, u_copy), 0)
    for k in (1, 2):
        loads[k].wait()
    build_counts()
    for k in range(3, len(loads)):
        loads[k].wait()
    pre = pre_ref[...]
    scale = jnp.ones((1, 1), F32)
    u = v
    overlap = jnp.zeros((1, 1), F32)
    square = overlap

    def total(rows):
        return jnp.sum(rows, axis=1, keepdims=True)

    for i in range(ITERS + 1):
        if i < ITERS:
            arrive((x_copy, u_copy), i)
        else:
            arrive((u_copy,), i)
        rows = jnp.sum(ubuf[i], axis=0)
        usq = total(rows[0:1])
        if i > 0:
            quotient = (overlap + total(rows[1:2])) / square
            if i == 1:
                first_ref[0] = jnp.sum(quotient)
            else:
                later_ref[i - 2] = jnp.sum(quotient)
            scale = lax.rsqrt(usq * (1.0 / entries) + 1e-06)
        if i == ITERS:
            break
        v = u * scale
        square = usq * scale * scale
        acc = apply(i)
        dots = jnp.zeros((own, br), F32)
        for o in range(n):
            t, h = o // per, o % per
            steps = own // SUB
            piece = jnp.concatenate(
                [acc[t * SUB:(t + 1) * SUB, (h * steps + a) * br:(h * steps + a + 1) * br]
                 for a in range(steps)], axis=0)
            rsend[i, o] = piece.astype(BF16)
            dots = dots + piece * xbuf[i, o].astype(F32)
        row = jnp.sum(dots, axis=0, keepdims=True)
        qsend[i] = row
        qbuf[i, me] = row
        rbuf[i, me] = rsend[i, me]
        start((r_copy, q_copy), i)
        arrive((r_copy, q_copy), i)
        w = jnp.zeros((own, br), F32)
        for o in range(n):
            w = w + rbuf[i, o].astype(F32)
        w = w * scale
        overlap = total(jnp.sum(qbuf[i], axis=0)) * scale * scale
        q = overlap / square
        missing = jnp.sum((v - scale * ub.astype(F32)) * w, axis=0, keepdims=True)
        u = v - pre * (w - q * v)
        ub = u.astype(BF16)
        offer(i + 1, u, missing)
        if i + 1 < ITERS:
            offer_x(i + 1, ub)
            start((x_copy, u_copy), i + 1)
        else:
            start((u_copy,), i + 1)
            part[...] = lax.dot_general(
                rot_ref[...], u, (((0,), (0,)), ((), ())),
                precision=lax.Precision.HIGHEST, preferred_element_type=F32)
            parity = lax.rem(me, 2)
            half = part.shape[0] // 2
            give = copy(part.at[pl.ds(pl.multiple_of((1 - parity) * half, half), half)],
                        got, p_out, p_in, me + 1 - 2 * parity)
            give.start()

    give.wait_recv()
    keep = part[pl.ds(pl.multiple_of(parity * half, half), half)]
    out_ref[...] = (keep + got[...]) * scale
    give.wait_send()
    for i in range(ITERS):
        sent((x_copy, u_copy, r_copy, q_copy), i)
    sent((u_copy,), ITERS)


def dense_body(psi_start, precond, left_ops, right_ops, term_in, term_out, term_live, left_rot):
    n = lax.axis_size("ops")
    slots, bl = left_ops.shape[0], left_ops.shape[1]
    own, br = psi_start.shape
    kept = left_rot.shape[1]
    sectors = n * own // bl
    st = sectors * SUB
    vmem = pl.BlockSpec(memory_space=pltpu.VMEM)
    smem = pl.BlockSpec(memory_space=pltpu.SMEM)
    dma = pltpu.SemaphoreType.DMA
    loaded = (psi_start, term_in, term_out, left_ops, right_ops, precond, left_rot)
    return pl.pallas_call(
        functools.partial(kernel, n),
        out_shape=(
            jax.ShapeDtypeStruct((1,), F32),
            jax.ShapeDtypeStruct((ITERS - 1,), F32),
            jax.ShapeDtypeStruct((kept // 2, br), F32),
        ),
        in_specs=[smem] + [pl.BlockSpec(memory_space=pl.ANY)] * 7,
        out_specs=(smem, smem, vmem),
        scratch_shapes=[pltpu.VMEM(a.shape, a.dtype) for a in loaded] + [
            dma((len(loaded),)),
            pltpu.VMEM((st, slots * 2 * st), BF16),
            pltpu.VMEM((slots * bl, sectors * br), BF16),
            pltpu.VMEM((slots * 2 * st, bl // SUB * br), BF16),
            pltpu.VMEM((ITERS, own, br), BF16),
            pltpu.VMEM((ITERS, n, own, br), BF16),
            pltpu.VMEM((ITERS, n, own, br), BF16),
            pltpu.VMEM((ITERS, n, own, br), BF16),
            pltpu.VMEM((ITERS, 1, br), F32),
            pltpu.VMEM((ITERS, n, 1, br), F32),
            pltpu.VMEM((ITERS + 1, 2, br), F32),
            pltpu.VMEM((ITERS + 1, n, 2, br), F32),
            pltpu.VMEM((kept, br), F32),
            pltpu.VMEM((kept // 2, br), F32),
            dma((ITERS, n)), dma((ITERS, n)), dma((ITERS, n)), dma((ITERS, n)),
            dma((ITERS, n)), dma((ITERS, n)), dma((ITERS + 1, n)), dma((ITERS + 1, n)),
            dma, dma,
        ],
        compiler_params=pltpu.CompilerParams(
            collective_id=0, has_side_effects=True, vmem_limit_bytes=60 * 2**20),
    )(term_live, *loaded)


def body(psi_start, precond, left_ops, right_ops, term_in, term_out, term_live, left_rot):
    n = lax.axis_size("ops")
    own = psi_start.shape[0]
    bl = left_ops.shape[1]
    sectors = n * own // bl
    dense = sectors <= term_in.shape[1] and own % SUB == 0 and bl == 2 * own
    run = dense_body if dense else pair_body
    return run(psi_start, precond, left_ops, right_ops, term_in, term_out, term_live, left_rot)


def solution(mesh):
    rows = P(("groups", "ops"), None)
    blocks = P(("groups", "ops"), None, None)
    return jax.shard_map(
        body,
        mesh=mesh,
        in_specs=(rows, rows, blocks, blocks, rows, rows, P(("groups", "ops")), rows),
        out_specs=(P("groups"), P("groups"), rows),
        check_vma=False,
    )
```
